32 devices in a mesh: row: 4 (over z), col: 8 (over y, x, core).
Axes of the slice: x: 2, y: 2, z: 4, core: 2. Of those that a mesh axis runs over, the one named last changes fastest.
Arguments:
- layer_input: bfloat16 [2, 4, 1024, 1792], P(None, 'row', 'col'), may hold values from -6 to 6
- cotangent: bfloat16 [2, 4, 1024, 1792], P(None, 'row', 'col'), may hold values from -6 to 6
- segments: int32 [2, 4, 1024], P(None, 'row'), may hold values from 0 to 1, never falling along the last dimension, each value on 1 to 768 neighbouring positions
- norm_gains: float32 [2, 1792], replicated, may hold values from 0.5 to 1.5
- gain_mean: float32 [2, 1792], replicated, may hold values from -56 to 56
- gain_square: float32 [2, 1792], replicated, may hold values from 409.6 to 1638.4
- conv_kernel: float32 [3, 1792], P(None, 'col'), may hold values from -4 to 4
- conv_mean: float32 [3, 1792], P(None, 'col'), may hold values from -56 to 56
- conv_square: float32 [3, 1792], P(None, 'col'), may hold values from 409.6 to 1638.4
- mix_weight: float32 [1792, 16, 256], P('row', 'col'), may hold values from -0.125 to 0.125
- mix_mean: float32 [1792, 16, 256], P('row', 'col'), may hold values from -56 to 56
- mix_square: float32 [1792, 16, 256], P('row', 'col'), may hold values from 409.6 to 1638.4
- out_weight: float32 [1792, 1792], P('col', 'row'), may hold values from -1 to 1
- out_mean: float32 [1792, 1792], P('col', 'row'), may hold values from -6 to 6
- out_square: float32 [1792, 1792], P('col', 'row'), may hold values from 1.6 to 6.4
- up_weight: float32 [2, 4864, 1792], P(None, ('row', 'col')), may hold values from -0.125 to 0.125
- up_mean: float32 [2, 4864, 1792], P(None, ('row', 'col')), may hold values from -20 to 20
- up_square: float32 [2, 4864, 1792], P(None, ('row', 'col')), may hold values from 49.152 to 196.608
- down_weight: float32 [4864, 1792], P(('row', 'col')), may hold values from -0.078125 to 0.078125
- down_mean: float32 [4864, 1792], P(('row', 'col')), may hold values from -32 to 32
- down_square: float32 [4864, 1792], P(('row', 'col')), may hold values from 147.456 to 589.824
Outputs:
- layer_output: bfloat16 [2, 4, 1024, 1792], P(None, 'row', 'col')
- input_grad: float32 [2, 4, 1024, 1792], P(None, 'row', 'col')
- gain_means: float32 [2, 1792], replicated
- gain_squares: float32 [2, 1792], replicated
- new_gains: float32 [2, 1792], replicated
- conv_means: float32 [3, 1792], P(None, 'col')
- conv_squares: float32 [3, 1792], P(None, 'col')
- new_kernel: float32 [3, 1792], P(None, 'col')
- mix_means: float32 [1792, 16, 256], P('row', 'col')
- mix_squares: float32 [1792, 16, 256], P('row', 'col')
- new_mix: float32 [1792, 16, 256], P('row', 'col')
- mix_copy: bfloat16 [1792, 16, 256], P('row', 'col')
- out_means: float32 [1792, 1792], P('col', 'row')
- out_squares: float32 [1792, 1792], P('col', 'row')
- new_out: float32 [1792, 1792], P('col', 'row')
- out_copy: bfloat16 [1792, 1792], P('col', 'row')
- up_means: float32 [2, 4864, 1792], P(None, ('row', 'col'))
- up_squares: float32 [2, 4864, 1792], P(None, ('row', 'col'))
- new_up: float32 [2, 4864, 1792], P(None, ('row', 'col'))
- up_copy: bfloat16 [2, 4864, 1792], P(None, ('row', 'col'))
- down_means: float32 [4864, 1792], P(('row', 'col'))
- down_squares: float32 [4864, 1792], P(('row', 'col'))
- new_down: float32 [4864, 1792], P(('row', 'col'))
- down_copy: bfloat16 [4864, 1792], P(('row', 'col'))
The draws below stay inside these ranges and needn't reach their ends.
Inputs may be any that keep to these rules, and one draw needn't show every extreme that they name: `segments`: along each sequence the document numbers never fall; each document holds 1 to 768 tokens.
All inputs are finite; a program needn't handle non-finite values.
Results may differ from the reference program's by a relative error of at most 0.025.
Values may be sent and summed in bfloat16 or wider, within the bound.
No kernel may reach another device: no remote copies, remote signals or barrier semaphores. Data moves between devices by JAX's collectives and lax.ppermute only.
A program may use at most 256 MiB of HBM per device.

```python
import math
import jax
import jax.numpy as jnp
import numpy as np
from jax import lax

D = 1792
H = 16
FEAT = 16
FF = 4864
KW = 3
SEQ_LEN = 1024
MICRO = 2
STEP = 10
PACK = 256
SEQS = 4
N_ROW = 4


def block_scale(own_key, shape, cuts, low, high):
    def one(position, blocks):
        steps = jax.random.uniform(jax.random.fold_in(jax.random.fold_in(own_key, 6), position), (blocks,), jnp.float32, low / len(cuts), high / len(cuts))
        return jnp.repeat(jnp.exp(steps), shape[position] // blocks).reshape((-1,) + (1,) * (len(shape) - position - 1))

    factor_of = one(*cuts[0])
    for cut in cuts[1:]:
        factor_of = factor_of * one(*cut)
    return factor_of


def profile(count, total, bound, slope):
    weights = [(1 << 20) // math.isqrt(standing ** slope) + 1 for standing in range(2, count + 1)]
    surplus, given = total - bound - (count - 1), [1] * (count - 1)
    while surplus > 0:
        movable = [i for i in range(count - 1) if given[i] < bound]
        pool, budget = sum([weights[i] for i in movable]), surplus
        for i in movable:
            extra = min(bound - given[i], max(1, budget * weights[i] // pool), surplus)
            given[i] = given[i] + extra
            surplus = surplus - extra
    return np.array([bound] + given)


def uneven_parts(key, number_of, total, most, skew):
    if number_of == 2:
        one = jax.random.randint(key, (), max(1, total - most), min(most, total - 1) + 1)
        return jnp.stack([one, total - one])
    lengths = jnp.asarray(profile(number_of, total, most, skew), jnp.int32)
    twos = (number_of - 1) // 2
    donor, sink = lengths[1:1 + 2 * twos:2], lengths[2:2 + 2 * twos:2]
    room = jnp.minimum(donor - 1, most - sink)
    moved = jax.random.randint(jax.random.fold_in(key, 1), (twos,), 0, 1 << 20) % (room + 1)
    lengths = lengths.at[1:1 + 2 * twos:2].set(donor - moved).at[2:2 + 2 * twos:2].set(sink + moved)
    return lengths[jax.random.permutation(jax.random.fold_in(key, 2), number_of)]


def gaussian(rng, extent, deviation, bound, split=(), held_as=jnp.bfloat16):
    level = block_scale(rng, extent, split, -0.22, 0.18) if split else 1.0
    array = jax.random.normal(rng, extent, jnp.float32) * deviation * level
    return jnp.minimum(jnp.maximum(array, -bound), bound).astype(held_as)


def setup_inputs(seed: int = 0) -> dict:
    arg_keys = jax.random.split(jax.random.key(seed), 22)
    return {
        "layer_input": gaussian(arg_keys[0], (MICRO, SEQS, SEQ_LEN, D), 1.0, 6.0, ((1, 4), (2, 8))),
        "cotangent": gaussian(arg_keys[1], (MICRO, SEQS, SEQ_LEN, D), 1.0, 6.0, ((1, 4), (2, 8))),
        "segments": jax.vmap(lambda own: jnp.searchsorted(jnp.cumsum(uneven_parts(own, max(2, SEQ_LEN // 400), SEQ_LEN, SEQ_LEN * 3 // 4, 2)), jnp.arange(SEQ_LEN), side="right"))(jax.random.split(arg_keys[2], MICRO * SEQS)).reshape((MICRO, SEQS, SEQ_LEN)).astype(jnp.int32),
        "norm_gains": jnp.clip(1.0 + 0.1 * jax.random.normal(arg_keys[3], (2, D), jnp.float32), 0.5, 1.5),
        "gain_mean": gaussian(arg_keys[4], (2, D), (0.1 * (MICRO * N_ROW * SEQ_LEN) ** 0.5), 56.0, (), jnp.float32),
        "gain_square": jnp.clip(jnp.exp(jax.random.uniform(arg_keys[5], (2, D), jnp.float32, math.log(409.6), math.log(1638.4))), 409.6, 1638.4),
        "conv_kernel": gaussian(arg_keys[6], (KW, D), 1.0, 4.0, ((1, 8),), jnp.float32),
        "conv_mean": gaussian(arg_keys[7], (KW, D), (0.1 * (MICRO * N_ROW * SEQ_LEN) ** 0.5), 56.0, ((1, 8),), jnp.float32),
        "conv_square": jnp.clip(jnp.exp(math.log(1638.4) - 1.3862944 * jax.random.uniform(arg_keys[8], (KW, D), jnp.float32) ** block_scale(arg_keys[8], (KW, D), ((1, 8),), -0.2, 0.2)), 409.6, 1638.4),
        "mix_weight": gaussian(arg_keys[9], (D, H, PACK), D ** -0.5, 0.125, ((0, 4), (1, 8)), jnp.float32),
        "mix_mean": gaussian(arg_keys[10], (D, H, PACK), (0.1 * (MICRO * N_ROW * SEQ_LEN) ** 0.5), 56.0, ((0, 4), (1, 8)), jnp.float32),
        "mix_square": jnp.clip(jnp.exp(math.log(1638.4) - 1.3862944 * jax.random.uniform(arg_keys[11], (D, H, PACK), jnp.float32) ** block_scale(arg_keys[11], (D, H, PACK), ((0, 4), (1, 8)), -0.2, 0.2)), 409.6, 1638.4),
        "out_weight": gaussian(arg_keys[12], (D, D), (D // 64) ** -0.5, 1.0, ((0, 8), (1, 4)), jnp.float32),
        "out_mean": gaussian(arg_keys[13], (D, D), (0.2 * (MICRO * N_ROW) ** 0.5), 6.0, ((0, 8), (1, 4)), jnp.float32),
        "out_square": jnp.clip(jnp.exp(math.log(6.4) - 1.3862944 * jax.random.uniform(arg_keys[14], (D, D), jnp.float32) ** block_scale(arg_keys[14], (D, D), ((0, 8), (1, 4)), -0.2, 0.2)), 1.6, 6.4),
        "up_weight": gaussian(arg_keys[15], (2, FF, D), D ** -0.5, 0.125, ((1, 32),), jnp.float32),
        "up_mean": gaussian(arg_keys[16], (2, FF, D), (0.035 * (MICRO * N_ROW * SEQ_LEN) ** 0.5), 20.0, ((1, 32),), jnp.float32),
        "up_square": jnp.clip(jnp.exp(math.log(196.608) - 1.3862944 * jax.random.uniform(arg_keys[17], (2, FF, D), jnp.float32) ** block_scale(arg_keys[17], (2, FF, D), ((1, 32),), -0.2, 0.2)), 49.152, 196.608),
        "down_weight": gaussian(arg_keys[18], (FF, D), FF ** -0.5, 0.078125, ((0, 32),), jnp.float32),
        "down_mean": gaussian(arg_keys[19], (FF, D), (0.06 * (MICRO * N_ROW * SEQ_LEN) ** 0.5), 32.0, ((0, 32),), jnp.float32),
        "down_square": jnp.clip(jnp.exp(math.log(589.824) - 1.3862944 * jax.random.uniform(arg_keys[20], (FF, D), jnp.float32) ** block_scale(arg_keys[20], (FF, D), ((0, 32),), -0.2, 0.2)), 147.456, 589.824),
    }


@jax.custom_vjp
def low(v):
    return lax.optimization_barrier(v.astype(jnp.bfloat16)).astype(jnp.float32)

@jax.custom_vjp
def low_back(v):
    return v

def low_keep(v):
    return (low(v), None)

def low_pass(kept, grad):
    return (grad,)

def back_keep(v):
    return (v, None)

def back_low(kept, grad):
    return (low(grad),)
low.defvjp(low_keep, low_pass)
low_back.defvjp(back_keep, back_low)
NORM_EPSILON = 1e-05
BETA_ONE = 0.9
BETA_TWO = 0.95
ADAM_EPSILON = 1e-08
DECAY_RATE = 0.1
VECTOR_RATE = 0.5
HIGHEST_PRECISION = lax.Precision.HIGHEST

def silu(tensor):
    return tensor * jax.nn.sigmoid(tensor)

def rms_norm(tensor, gain):
    scale = lax.rsqrt(lax.optimization_barrier(jnp.mean(tensor * tensor, axis=-1, keepdims=True)) + NORM_EPSILON)
    return tensor * scale * gain

def shift_down(tensor, offset):
    filler = jnp.zeros((offset,) + tensor.shape[1:], tensor.dtype)
    return jnp.concatenate([filler, tensor[:tensor.shape[0] - offset]], axis=0)

def same_segment(segs, offset):
    earlier = jnp.concatenate([jnp.full((offset,), -1, jnp.int32), segs[:segs.shape[0] - offset].astype(jnp.int32)])
    return (earlier == segs.astype(jnp.int32)).astype(jnp.float32)

def layer(input_seq, params, segs):
    gains, kernel, mix_w, out_w, up_w, down_w = params
    length = input_seq.shape[0]
    block_rows = min(512, length)
    block_count = length // block_rows
    feat_root = math.sqrt(FEAT)
    head_dim = D // H
    pack_dim = 2 * FEAT + 2 * head_dim
    normed = low(rms_norm(input_seq, gains[0]))
    projected = jnp.dot(normed, low(mix_w).reshape(D, H * pack_dim), precision=HIGHEST_PRECISION)
    projected = low_back(projected).reshape(length, H, pack_dim)
    queries = low(projected[:, :, :FEAT])
    key_rows = low(projected[:, :, FEAT:2 * FEAT])
    inner_vals = projected[:, :, 2 * FEAT:2 * FEAT + head_dim]
    gate_mix = projected[:, :, 2 * FEAT + head_dim:]
    kernel_taps = kernel.reshape(KW, H, head_dim)
    convolved = kernel_taps[0] * inner_vals
    for offset in range(1, KW):
        convolved = convolved + kernel_taps[offset] * shift_down(inner_vals, offset) * same_segment(segs, offset)[:, None, None]
    values = low(convolved * silu(gate_mix))
    positions = jnp.arange(length, dtype=jnp.int32)

    def attend(block_index):
        first_row = block_index * block_rows
        query_block = lax.dynamic_slice_in_dim(queries, first_row, block_rows, 0)
        seg_block = lax.dynamic_slice_in_dim(segs, first_row, block_rows, 0)
        pos_block = first_row + jnp.arange(block_rows, dtype=jnp.int32)
        scores = low_back(jnp.einsum('thf,rhf->htr', query_block, key_rows, precision=HIGHEST_PRECISION) / feat_root)
        key_mask = (pos_block[:, None] >= positions[None, :]) & (seg_block[:, None] == segs[None, :])
        kern = jnp.where(key_mask[None], 1.0 + scores + 0.5 * scores * scores, 0.0)
        row_total = lax.optimization_barrier(jnp.sum(kern, axis=2, keepdims=True))
        weights = low(kern / row_total)
        return jnp.einsum('htr,rhe->the', weights, values, precision=HIGHEST_PRECISION)
    attended = lax.map(jax.checkpoint(attend), jnp.arange(block_count, dtype=jnp.int32))
    attended = low(low_back(attended.reshape(length, D)))
    mixer_sum = low_back(jnp.dot(attended, low(out_w), precision=HIGHEST_PRECISION))
    resid = input_seq + mixer_sum
    normed_two = low(rms_norm(resid, gains[1]))
    up_flat = low(up_w).reshape(2 * FF, D)
    gate_up = low_back(jnp.dot(normed_two, up_flat.T, precision=HIGHEST_PRECISION)).reshape(length, 2, FF)
    hidden = low(silu(gate_up[:, 0]) * gate_up[:, 1])
    ffn_sum = low_back(jnp.dot(hidden, low(down_w), precision=HIGHEST_PRECISION))
    return resid + ffn_sum

def adam_update(weight, gradient, moment_one, moment_two, step_rate, decay_rate):
    first_new = BETA_ONE * moment_one + (1.0 - BETA_ONE) * gradient
    second_new = BETA_TWO * moment_two + (1.0 - BETA_TWO) * gradient * gradient
    first_hat = first_new / (1.0 - BETA_ONE ** STEP)
    second_hat = second_new / (1.0 - BETA_TWO ** STEP)
    weight_new = weight - step_rate * (first_hat / (jnp.sqrt(second_hat) + ADAM_EPSILON) + decay_rate * weight)
    return (first_new, second_new, weight_new)

def reference(layer_input, cotangent, segments, norm_gains, gain_mean, gain_square, conv_kernel, conv_mean, conv_square, mix_weight, mix_mean, mix_square, out_weight, out_mean, out_square, up_weight, up_mean, up_square, down_weight, down_mean, down_square):
    params = (norm_gains, conv_kernel, mix_weight, out_weight, up_weight, down_weight)
    seq_count = MICRO * SEQS
    inputs_all = layer_input.reshape(seq_count, SEQ_LEN, D).astype(jnp.float32)
    cot_all = cotangent.reshape(seq_count, SEQ_LEN, D).astype(jnp.float32)
    segs_all = segments.reshape(seq_count, SEQ_LEN).astype(jnp.int32)

    def one_seq(running, batch_item):
        input_seq, cot_seq, segs = batch_item

        def forward(tensor, weights):
            return layer(tensor, weights, segs)
        result, pull = jax.vjp(forward, input_seq, params)
        grad_input, grad_params = pull(cot_seq)
        running = jax.tree.map(jnp.add, running, grad_params)
        return (running, (result.astype(jnp.bfloat16), grad_input))
    zero_grads = jax.tree.map(jnp.zeros_like, params)
    grad_sums, (outputs, grads_input) = lax.scan(one_seq, zero_grads, (inputs_all, cot_all, segs_all))
    grad_gains, grad_kernel, grad_mix, grad_out, grad_up, grad_down = grad_sums
    gain_means, gain_squares, new_gains = adam_update(norm_gains, grad_gains, gain_mean, gain_square, VECTOR_RATE, 0.0)
    conv_means, conv_squares, new_kernel = adam_update(conv_kernel, grad_kernel, conv_mean, conv_square, VECTOR_RATE, 0.0)
    mix_means, mix_squares, new_mix = adam_update(mix_weight, grad_mix, mix_mean, mix_square, D ** (-0.5), DECAY_RATE)
    out_means, out_squares, new_out = adam_update(out_weight, grad_out, out_mean, out_square, 8.0 * D ** (-0.5), DECAY_RATE)
    up_means, up_squares, new_up = adam_update(up_weight, grad_up, up_mean, up_square, D ** (-0.5), DECAY_RATE)
    down_means, down_squares, new_down = adam_update(down_weight, grad_down, down_mean, down_square, FF ** (-0.5), DECAY_RATE)
    layer_output = outputs.reshape(MICRO, SEQS, SEQ_LEN, D)
    input_grad = grads_input.reshape(MICRO, SEQS, SEQ_LEN, D)
    return (layer_output, input_grad, gain_means, gain_squares, new_gains, conv_means, conv_squares, new_kernel, mix_means, mix_squares, new_mix, new_mix.astype(jnp.bfloat16), out_means, out_squares, new_out, new_out.astype(jnp.bfloat16), up_means, up_squares, new_up, new_up.astype(jnp.bfloat16), down_means, down_squares, new_down, new_down.astype(jnp.bfloat16))
```

```python
import functools
import math

import jax
import jax.numpy as jnp
from jax import lax
from jax.experimental import pallas as pl
from jax.experimental.pallas import tpu as pltpu
from jax.sharding import PartitionSpec as P

D = 1792
FF = 4864
STEP = 10


NORM_EPSILON = 1e-05
BETA_ONE = 0.9
BETA_TWO = 0.95
ADAM_EPSILON = 1e-08
DECAY_RATE = 0.1
VECTOR_RATE = 0.5

LANES = 128
BLOCK_T = 256


def silu_grad(tensor):
    sigmoid_val = jax.nn.sigmoid(tensor)
    return sigmoid_val * (1.0 + tensor * (1.0 - sigmoid_val))


def low(tensor):
    return tensor.astype(jnp.bfloat16)


def wide(tensor):
    return tensor.astype(jnp.float32)


def dot_nn(left_side, right_side):
    return lax.dot_general(
        left_side, right_side, (((1,), (0,)), ((), ())), preferred_element_type=jnp.float32
    )


def dot_tn(left_side, right_side):
    return lax.dot_general(
        left_side, right_side, (((0,), (0,)), ((), ())), preferred_element_type=jnp.float32
    )


def dot_nt(left_side, right_side):
    return lax.dot_general(
        left_side, right_side, (((1,), (1,)), ((), ())), preferred_element_type=jnp.float32
    )


def row_scale(tensor):
    return lax.rsqrt(jnp.mean(tensor * tensor, axis=1, keepdims=True) + NORM_EPSILON)


def adam_update(weight, gradient, moment_one, moment_two, step_rate, decay_rate):
    first_new = BETA_ONE * moment_one + (1.0 - BETA_ONE) * gradient
    second_new = BETA_TWO * moment_two + (1.0 - BETA_TWO) * gradient * gradient
    first_hat = first_new / (1.0 - BETA_ONE**STEP)
    second_hat = second_new / (1.0 - BETA_TWO**STEP)
    weight_new = weight - step_rate * (
        first_hat / (jnp.sqrt(second_hat) + ADAM_EPSILON) + decay_rate * weight
    )
    return (first_new, second_new, weight_new)


def col_masks(col_count, core):
    bits = [1 << place for place in range(1, col_count.bit_length() - 1)]
    return bits if core == 0 else bits[::-1]


def chip_perm(col_count, step):
    return [(i, i ^ col_masks(col_count, i & 1)[step]) for i in range(col_count)]


def core_perm(col_count):
    return [(i, i ^ 1) for i in range(col_count)]


def col_steps(col_count):
    return col_count.bit_length() - 2


def slots_of_chunks(col_count):
    table = []
    for me in range(col_count):
        row = [0] * col_count
        for half in range(2):
            origin = me ^ half
            masks = col_masks(col_count, origin & 1)
            for slot in range(col_count // 2):
                chunk = origin
                for step, mask in enumerate(masks):
                    if slot >> step & 1:
                        chunk ^= mask
                row[chunk] = half * (col_count // 2) + slot
        table.append(row)
    return jnp.asarray(table, jnp.int32)[lax.axis_index("col")]


class Line:
    def __init__(self):
        self.marks = ()

    def hold(self, *arrays):
        return lax.optimization_barrier(arrays + self.marks)[: len(arrays)]

    def mark(self, *arrays):
        self.marks = arrays


class Stage:
    def __init__(self, steps):
        self.steps, self.ended, self.result = steps, False, None
        self.advance()

    def advance(self):
        if not self.ended:
            try:
                next(self.steps)
            except StopIteration as stop:
                self.ended, self.result = True, stop.value


def advance(*stages):
    for stage in stages:
        stage.advance()


def finish(stage):
    while not stage.ended:
        stage.advance()
    return stage.result


def gather_col(line, part, col_count):
    (held,) = line.hold(part)
    line.mark(held)
    arrived = lax.ppermute(held, "col", chip_perm(col_count, 0))
    for step in range(1, col_steps(col_count)):
        yield
        (arrived,) = line.hold(arrived)
        held = jnp.concatenate([held, arrived], axis=0)
        line.mark(held)
        arrived = lax.ppermute(held, "col", chip_perm(col_count, step))
    other_held = lax.ppermute(held, "col", core_perm(col_count))
    yield
    (arrived,) = line.hold(arrived)
    line.mark(arrived)
    other_arrived = lax.ppermute(arrived, "col", core_perm(col_count))
    yield
    other_held, other_arrived = line.hold(other_held, other_arrived)
    line.mark(other_held, other_arrived)
    return [held, arrived, other_held, other_arrived]


def scatter_col(line, own, other, col_count):
    line.mark(own, other)
    arrived = lax.ppermute(other, "col", core_perm(col_count))
    last_step = col_steps(col_count) - 1
    yield
    (arrived,) = line.hold(arrived)
    upper = low(wide(own[1]) + wide(arrived[1]))
    line.mark(upper)
    lower = arrived[0]
    arrived = lax.ppermute(upper, "col", chip_perm(col_count, last_step))
    yield
    arrived, lower = line.hold(arrived, lower)
    total = wide(own[0]) + wide(lower) + wide(arrived)
    for step in reversed(range(last_step)):
        rows = total.shape[0] // 2
        send = low(total[rows:])
        line.mark(send)
        arrived = lax.ppermute(send, "col", chip_perm(col_count, step))
        yield
        (arrived,) = line.hold(arrived)
        total = wide(total[:rows]) + wide(arrived)
    return total


def sum_over(tensor, axis, count):
    bit = 1
    while bit < count:
        tensor = tensor + lax.ppermute(tensor, axis, [(i, i ^ bit) for i in range(count)])
        bit *= 2
    return tensor


def head_parts(feat_dim, head_dim, inv_ref, proj_ref, taps_ref, link_ref, p_ref):
    length = p_ref.shape[0]
    chunks = inv_ref.shape[0]
    rows = length // chunks
    for chunk in range(chunks):
        source = pl.multiple_of(inv_ref[chunk] * rows, rows)
        p_ref[chunk * rows : (chunk + 1) * rows, :] = proj_ref[pl.ds(source, rows), :]
    packed = p_ref[...]
    pack_dim = packed.shape[1]
    lane = lax.broadcasted_iota(jnp.int32, (length, LANES), 1)
    first = packed[:, :LANES]
    queries = low(jnp.where(lane < feat_dim, first, 0.0))
    keys = low(jnp.where(lane < feat_dim, pltpu.roll(first, LANES - feat_dim, 1), 0.0))
    inner = pltpu.roll(packed, pack_dim - 2 * feat_dim, 1)[:, :LANES]
    inner = jnp.where(lane < head_dim, inner, 0.0)
    gate = pltpu.roll(packed, pack_dim - 2 * feat_dim - head_dim, 1)[:, :LANES]
    gate = jnp.where(lane < head_dim, gate, 0.0)
    taps = taps_ref[0]
    shifted = [inner]
    conv = taps[0:1, :] * inner
    for offset in range(1, taps.shape[0]):
        moved = pltpu.roll(inner, offset, 0)
        shifted.append(moved)
        conv = conv + taps[offset : offset + 1, :] * (moved * link_ref[:, offset : offset + 1])
    return queries, keys, gate, taps, shifted, conv


def kept_scores(feat_dim, block, keys, queries, segc_ref, segr_ref):
    first, last = block * BLOCK_T, (block + 1) * BLOCK_T
    score = dot_nt(keys[:last], queries[first:last]) * (1.0 / math.sqrt(feat_dim))
    key_at = lax.broadcasted_iota(jnp.int32, (last, BLOCK_T), 0)
    query_at = first + lax.broadcasted_iota(jnp.int32, (last, BLOCK_T), 1)
    kept = (key_at <= query_at) & (segc_ref[:last, :] == segr_ref[:, first:last])
    kern = jnp.where(kept, 1.0 + score + 0.5 * score * score, 0.0)
    scale = 1.0 / jnp.sum(kern, axis=0, keepdims=True)
    return score, kept, kern * scale, scale


def forward_kernel(
    feat_dim, head_dim, inv_ref, proj_ref, taps_ref, link_ref, segc_ref, segr_ref, out_ref, p_ref
):
    queries, keys, gate, taps, shifted, conv = head_parts(
        feat_dim, head_dim, inv_ref, proj_ref, taps_ref, link_ref, p_ref
    )
    length = p_ref.shape[0]
    values = low(conv * (gate * jax.nn.sigmoid(gate))).T
    blocks = []
    for block in range(length // BLOCK_T):
        score, kept, probs, scale = kept_scores(
            feat_dim, block, keys, queries, segc_ref, segr_ref
        )
        last = (block + 1) * BLOCK_T
        blocks.append(low(dot_nn(values[:, :last], low(probs)).T))
    attended = jnp.concatenate(blocks, axis=0)
    chunks = inv_ref.shape[0]
    rows = length // chunks
    for chunk in range(chunks):
        target = pl.multiple_of(inv_ref[chunk] * rows, rows)
        out_ref[pl.ds(target, rows), :] = attended[chunk * rows : (chunk + 1) * rows]


def backward_kernel(
    feat_dim,
    head_dim,
    inv_ref,
    proj_ref,
    grad_ref,
    taps_ref,
    link_ref,
    segc_ref,
    segr_ref,
    out_ref,
    tap_ref,
    p_ref,
    g_ref,
    dk_ref,
    dv_ref,
):
    queries, keys, gate, taps, shifted, conv = head_parts(
        feat_dim, head_dim, inv_ref, proj_ref, taps_ref, link_ref, p_ref
    )
    length = p_ref.shape[0]
    chunks = inv_ref.shape[0]
    rows = length // chunks
    for chunk in range(chunks):
        source = pl.multiple_of(inv_ref[chunk] * rows, rows)
        g_ref[chunk * rows : (chunk + 1) * rows, :] = grad_ref[pl.ds(source, rows), :]
    grad = g_ref[...]
    sigmoid_val = jax.nn.sigmoid(gate)
    gate_act = gate * sigmoid_val
    values = low(conv * gate_act)
    keys_turned = keys.T
    root = 1.0 / math.sqrt(feat_dim)
    dk_ref[...] = jnp.zeros_like(dk_ref)
    dv_ref[...] = jnp.zeros_like(dv_ref)
    query_grads = []
    for block in range(length // BLOCK_T):
        first, last = block * BLOCK_T, (block + 1) * BLOCK_T
        score, kept, probs, scale = kept_scores(
            feat_dim, block, keys, queries, segc_ref, segr_ref
        )
        weight_grad = dot_nt(values[:last], grad[first:last])
        row_dot = jnp.sum(weight_grad * probs, axis=0, keepdims=True)
        score_grad = low(
            jnp.where(kept, (weight_grad - row_dot) * scale * (1.0 + score), 0.0)
        )
        query_grads.append(dot_nn(keys_turned[:, :last], score_grad).T)
        dk_ref[:last, :] += dot_nn(score_grad, queries[first:last])
        dv_ref[:last, :] += dot_nn(low(probs), grad[first:last])
    grad_queries = jnp.concatenate(query_grads, axis=0) * root
    grad_keys = dk_ref[...] * root
    grad_values = dv_ref[...]
    grad_conv = grad_values * gate_act
    grad_gate = grad_values * conv * (sigmoid_val * (1.0 + gate * (1.0 - sigmoid_val)))
    grad_inner = taps[0:1, :] * grad_conv
    tap_rows = [jnp.sum(grad_conv * shifted[0], axis=0, keepdims=True)]
    for offset in range(1, taps.shape[0]):
        masked = grad_conv * link_ref[:, offset : offset + 1]
        tap_rows.append(jnp.sum(masked * shifted[offset], axis=0, keepdims=True))
        grad_inner = grad_inner + taps[offset : offset + 1, :] * pltpu.roll(
            masked, length - offset, 0
        )
    for offset, tap_row in enumerate(tap_rows):
        tap_ref[0, offset : offset + 1, :] = tap_row
    empty = jnp.zeros((length, LANES), jnp.float32)
    packed = jnp.concatenate([grad_queries + pltpu.roll(grad_keys, feat_dim, 1), empty], axis=1)
    packed = packed + pltpu.roll(jnp.concatenate([grad_inner, empty], axis=1), 2 * feat_dim, 1)
    packed = low(
        packed
        + pltpu.roll(jnp.concatenate([grad_gate, empty], axis=1), 2 * feat_dim + head_dim, 1)
    )
    for chunk in range(chunks):
        target = pl.multiple_of(inv_ref[chunk] * rows, rows)
        out_ref[pl.ds(target, rows), :] = packed[chunk * rows : (chunk + 1) * rows]


def whole_spec(shape):
    return pl.BlockSpec(shape, lambda head, inv: (0,) * len(shape))


def attend(inv, projected, taps, links, segc, segr, feat_dim, head_dim):
    length = projected.shape[0]
    heads, tap_count = taps.shape[0], taps.shape[1]
    pack_dim = projected.shape[1] // heads
    return pl.pallas_call(
        functools.partial(forward_kernel, feat_dim, head_dim),
        out_shape=jax.ShapeDtypeStruct((length, heads * LANES), jnp.bfloat16),
        grid_spec=pltpu.PrefetchScalarGridSpec(
            num_scalar_prefetch=1,
            grid=(heads,),
            in_specs=[
                pl.BlockSpec((length, pack_dim), lambda head, inv: (0, head)),
                pl.BlockSpec((1, tap_count, LANES), lambda head, inv: (head, 0, 0)),
                whole_spec(links.shape),
                whole_spec(segc.shape),
                whole_spec(segr.shape),
            ],
            out_specs=pl.BlockSpec((length, LANES), lambda head, inv: (0, head)),
            scratch_shapes=[pltpu.VMEM((length, pack_dim), jnp.float32)],
        ),
        compiler_params=pltpu.CompilerParams(vmem_limit_bytes=40 * 1024 * 1024),
        cost_estimate=pl.CostEstimate(
            flops=heads * length * length * LANES * 3,
            bytes_accessed=heads * length * (pack_dim * 4 + LANES * 2),
            transcendentals=heads * length * LANES,
        ),
    )(inv, projected, taps, links, segc, segr)


def attend_back(inv, projected, grad, taps, links, segc, segr, feat_dim, head_dim):
    length = projected.shape[0]
    heads, tap_count = taps.shape[0], taps.shape[1]
    pack_dim = projected.shape[1] // heads
    return pl.pallas_call(
        functools.partial(backward_kernel, feat_dim, head_dim),
        out_shape=(
            jax.ShapeDtypeStruct((length, heads * pack_dim), jnp.bfloat16),
            jax.ShapeDtypeStruct((heads, tap_count, LANES), jnp.float32),
        ),
        grid_spec=pltpu.PrefetchScalarGridSpec(
            num_scalar_prefetch=1,
            grid=(heads,),
            in_specs=[
                pl.BlockSpec((length, pack_dim), lambda head, inv: (0, head)),
                pl.BlockSpec((length, LANES), lambda head, inv: (0, head)),
                pl.BlockSpec((1, tap_count, LANES), lambda head, inv: (head, 0, 0)),
                whole_spec(links.shape),
                whole_spec(segc.shape),
                whole_spec(segr.shape),
            ],
            out_specs=(
                pl.BlockSpec((length, pack_dim), lambda head, inv: (0, head)),
                pl.BlockSpec((1, tap_count, LANES), lambda head, inv: (head, 0, 0)),
            ),
            scratch_shapes=[
                pltpu.VMEM((length, pack_dim), jnp.float32),
                pltpu.VMEM((length, LANES), jnp.bfloat16),
                pltpu.VMEM((length, LANES), jnp.float32),
                pltpu.VMEM((length, LANES), jnp.float32),
            ],
        ),
        compiler_params=pltpu.CompilerParams(vmem_limit_bytes=48 * 1024 * 1024),
        cost_estimate=pl.CostEstimate(
            flops=heads * length * length * LANES * 6,
            bytes_accessed=heads * length * (pack_dim * 6 + LANES * 2),
            transcendentals=heads * length * LANES,
        ),
    )(inv, projected, grad, taps, links, segc, segr)


def ffn_kernel(*refs):
    normed_refs, cot_refs = refs[:4], refs[4:8]
    weight_ref, turned_ref, own_ref, other_ref = refs[8:]
    hidden, width = weight_ref.shape[1:]
    rows = normed_refs[0].shape[0]
    normed = jnp.concatenate([ref[...] for ref in normed_refs], axis=0)
    cot = jnp.concatenate([ref[...] for ref in cot_refs], axis=0)
    gate = dot_nt(weight_ref[0], normed)
    up = dot_nt(weight_ref[1], normed)
    grad_hidden = dot_nt(weight_ref[2], cot)
    sigmoid_val = jax.nn.sigmoid(gate)
    gate_sig = gate * sigmoid_val
    turned_ref[0] = low(grad_hidden * up * (sigmoid_val * (1.0 + gate * (1.0 - sigmoid_val))))
    turned_ref[1] = low(grad_hidden * gate_sig)
    turned_ref[2] = low(gate_sig * up)
    back = low(
        dot_tn(
            turned_ref[:2].reshape(2 * hidden, 4 * rows), weight_ref[:2].reshape(2 * hidden, width)
        )
    )
    for block, ref in enumerate((own_ref, own_ref, other_ref, other_ref)):
        ref[block % 2] = back[block * rows : (block + 1) * rows]


def ffn_call(normed, cot, weights):
    block_rows, width = normed[0].shape
    _, hidden, _ = weights.shape
    rows = block_rows // 2
    block = pl.BlockSpec((rows, width), lambda step: (step, 0))
    half = pl.BlockSpec((2, rows, width), lambda step: (0, step, 0))
    return pl.pallas_call(
        ffn_kernel,
        grid=(block_rows // rows,),
        in_specs=[block] * 8
        + [
            pl.BlockSpec(
                weights.shape, lambda step: (0, 0, 0), pipeline_mode=pl.Buffered(buffer_count=1)
            )
        ],
        out_specs=(
            pl.BlockSpec((3, hidden, 4 * rows), lambda step: (0, 0, step)),
            half,
            half,
        ),
        out_shape=(
            jax.ShapeDtypeStruct((3, hidden, 4 * block_rows), jnp.bfloat16),
            jax.ShapeDtypeStruct((2, block_rows, width), jnp.bfloat16),
            jax.ShapeDtypeStruct((2, block_rows, width), jnp.bfloat16),
        ),
        compiler_params=pltpu.CompilerParams(vmem_limit_bytes=52 * 1024 * 1024),
        cost_estimate=pl.CostEstimate(
            flops=2 * 5 * 4 * block_rows * hidden * width,
            bytes_accessed=2 * (3 * hidden * width + 12 * block_rows * width),
            transcendentals=4 * block_rows * hidden,
        ),
    )(*normed, *cot, weights)


def ffn_sum_kernel(hidden_ref, weight_ref, own_ref, other_ref):
    rows = own_ref.shape[1]
    total = low(dot_tn(hidden_ref[0], weight_ref[0]))
    for block, ref in enumerate((own_ref, own_ref, other_ref, other_ref)):
        ref[block % 2] = total[block * rows : (block + 1) * rows]


def ffn_sum_call(turned, weights):
    _, hidden, tokens = turned.shape
    width = weights.shape[2]
    rows = tokens // 8
    half = pl.BlockSpec((2, rows, width), lambda step: (0, step, 0))
    shape = jax.ShapeDtypeStruct((2, tokens // 4, width), jnp.bfloat16)
    return pl.pallas_call(
        ffn_sum_kernel,
        grid=(2,),
        in_specs=[
            pl.BlockSpec((1, hidden, 4 * rows), lambda step: (2, 0, step)),
            pl.BlockSpec((1, hidden, width), lambda step: (2, 0, 0)),
        ],
        out_specs=(half, half),
        out_shape=(shape, shape),
        compiler_params=pltpu.CompilerParams(vmem_limit_bytes=40 * 1024 * 1024),
        cost_estimate=pl.CostEstimate(
            flops=2 * tokens * hidden * width,
            bytes_accessed=2 * (hidden * width + tokens * (hidden + width)),
            transcendentals=0,
        ),
    )(turned, weights)


def ffn_grad_kernel(micro_count, steps, *refs):
    turned_refs, block_refs, out_ref = refs[:micro_count], refs[micro_count:-1], refs[-1]
    owners, kinds, own, _ = out_ref.shape
    hidden = owners * own
    rows = block_refs[0].shape[0] // steps
    total = None
    for micro, turned_ref in enumerate(turned_refs):
        tokens = jnp.concatenate(
            [
                ref[step * rows : (step + 1) * rows, :]
                for step in range(steps)
                for ref in block_refs[4 * micro : 4 * micro + 4]
            ],
            axis=0,
        )
        part = dot_nn(turned_ref[...].reshape(kinds * hidden, turned_ref.shape[2]), tokens)
        total = part if total is None else total + part
    for owner in range(owners):
        for kind in range(kinds):
            first = kind * hidden + owner * own
            out_ref[owner, kind] = low(total[first : first + own])


def ffn_grad_call(turned, blocks, first, kinds, owners):
    micro_count = len(turned)
    _, hidden, tokens = turned[0].shape
    block_rows, width = blocks[0][0].shape
    lanes = 2 * LANES
    return pl.pallas_call(
        functools.partial(ffn_grad_kernel, micro_count, 2),
        grid=(width // lanes,),
        in_specs=[
            pl.BlockSpec(
                (kinds, hidden, tokens),
                lambda step: (first // kinds, 0, 0),
                pipeline_mode=pl.Buffered(buffer_count=1),
            )
        ]
        * micro_count
        + [pl.BlockSpec((block_rows, lanes), lambda step: (0, step))] * (4 * micro_count),
        out_specs=pl.BlockSpec(
            (owners, kinds, hidden // owners, lanes), lambda step: (0, 0, 0, step)
        ),
        out_shape=jax.ShapeDtypeStruct((owners, kinds, hidden // owners, width), jnp.bfloat16),
        compiler_params=pltpu.CompilerParams(vmem_limit_bytes=52 * 1024 * 1024),
        cost_estimate=pl.CostEstimate(
            flops=2 * kinds * micro_count * tokens * hidden * width,
            bytes_accessed=2 * (kinds * hidden * (width + tokens) + micro_count * tokens * width),
            transcendentals=0,
        ),
    )(*turned, *[block for group in blocks for block in group])


def local(
    layer_input,
    cotangent,
    segments,
    norm_gains,
    gain_mean,
    gain_square,
    conv_kernel,
    conv_mean,
    conv_square,
    mix_weight,
    mix_mean,
    mix_square,
    out_weight,
    out_mean,
    out_square,
    up_weight,
    up_mean,
    up_square,
    down_weight,
    down_mean,
    down_square,
):
    micro_count = layer_input.shape[0]
    length = segments.shape[2]
    width_all = layer_input.shape[3]
    block_d, heads, pack_dim = mix_weight.shape
    width_col = out_weight.shape[0]
    head_dim = width_col // heads
    feat_dim = (pack_dim - 2 * head_dim) // 2
    tap_count = conv_kernel.shape[0]
    row_count = lax.axis_size("row")
    col_count = lax.axis_size("col")
    hidden_own = down_weight.shape[0]
    hidden_col = hidden_own * row_count
    row_me = lax.axis_index("row")
    inv = slots_of_chunks(col_count)
    micros = range(micro_count)
    gain_one, gain_two = norm_gains[0], norm_gains[1]

    mix_own = low(mix_weight).reshape(block_d, heads * pack_dim)
    out_own = jnp.pad(
        low(out_weight).reshape(heads, head_dim, block_d), ((0, 0), (0, LANES - head_dim), (0, 0))
    )
    out_own = out_own.reshape(heads * LANES, block_d).T
    mix_out_own = jnp.concatenate([mix_own, out_own], axis=1)
    mix_out = lax.all_gather(mix_out_own, "row", axis=0, tiled=True)
    mix_full, out_full = mix_out[:, : heads * pack_dim], mix_out[:, heads * pack_dim :]
    ffn_own = low(jnp.concatenate([up_weight, down_weight[None]], axis=0))
    ffn_full = lax.all_gather(ffn_own, "row", axis=1, tiled=True)

    taps = jnp.pad(
        conv_kernel.reshape(tap_count, heads, head_dim).transpose(1, 0, 2),
        ((0, 0), (0, 0), (0, LANES - head_dim)),
    )

    def links_of(segs):
        columns = [jnp.ones((length,), jnp.float32)]
        for offset in range(1, tap_count):
            earlier = jnp.concatenate(
                [jnp.full((offset,), -1, jnp.int32), segs[: length - offset]]
            )
            columns.append((earlier == segs).astype(jnp.float32))
        return jnp.stack(columns, axis=1)

    inputs = [wide(layer_input[m, 0]) for m in micros]
    scale_one = [row_scale(x) for x in inputs]
    norm_one = [x * s * gain_one for x, s in zip(inputs, scale_one)]
    cot_own = [wide(cotangent[m, 0]) for m in micros]
    segs = [segments[m, 0] for m in micros]
    links = [links_of(sg) for sg in segs]
    segc = [sg[:, None] for sg in segs]
    segr = [sg[None, :] for sg in segs]
    first, second = micros[0], micros[-1]
    line = Line()

    def col_gather(part):
        return Stage(gather_col(line, part, col_count))

    def col_scatter(own, other):
        return Stage(scatter_col(line, own, other, col_count))

    def halves(product):
        half, rows = length // 2, length // 4
        own, other = low(product(0, half)), low(product(half, length))
        return own.reshape(2, rows, width_all), other.reshape(2, rows, width_all)

    def joined(blocks):
        full = jnp.concatenate(blocks, axis=0)
        line.mark(full)
        return full

    def start_attention(m):
        normed, mix = line.hold(normed_one[m], mix_full)
        proj = dot_nn(normed, mix)
        att = attend(inv, proj, taps, links[m], segc[m], segr[m], feat_dim, head_dim)
        projected[m], attended[m] = proj, att
        return col_scatter(*halves(lambda lo, hi: dot_nt(att[lo:hi], out_full)))

    def end_mixer(m, stage):
        resid[m] = inputs[m] + finish(stage)
        scale_two[m] = row_scale(resid[m])
        norm_two[m] = resid[m] * scale_two[m] * gain_two
        return col_gather(low(norm_two[m]))

    normed_one, cots, projected, attended, resid, scale_two, norm_two, normed_two = [
        [None] * micro_count for _ in range(8)
    ]

    one_a = col_gather(low(norm_one[first]))
    line.mark(*line.marks, ffn_own)
    advance(one_a)
    one_b = col_gather(low(norm_one[second]))
    advance(one_b, one_a)
    cot_a = col_gather(cotangent[first, 0])
    normed_one[first] = joined(finish(one_a))
    advance(one_b, cot_a)
    normed_one[second] = joined(finish(one_b))
    mix_a = start_attention(first)
    advance(cot_a)
    cot_b = col_gather(cotangent[second, 0])
    mix_b = start_attention(second)
    advance(mix_a, cot_b, mix_b)
    cots[first] = finish(cot_a)
    advance(mix_a, cot_b, mix_b)
    two_a = end_mixer(first, mix_a)
    two_b = end_mixer(second, mix_b)
    advance(two_a)
    cots[second] = finish(cot_b)
    advance(two_b)
    advance(two_a)
    normed_two[first] = finish(two_a)
    advance(two_b)
    (ffn_full,) = line.hold(ffn_full)
    line.mark(ffn_full)
    normed_two[second] = finish(two_b)

    turned, resid_grad, outputs = [[None] * micro_count for _ in range(3)]

    def start_back(m):
        held = line.hold(*normed_two[m], *cots[m])
        turned[m], own, other = ffn_call(held[:4], held[4:], ffn_full)
        return col_scatter(own, other)

    def start_ffn_sum(m):
        (held,) = line.hold(turned[m])
        return col_scatter(*ffn_sum_call(held, ffn_full))

    gain_two_sum = 0.0

    def end_back(m, stage):
        back = finish(stage)
        mean_two = jnp.mean(back * norm_two[m], axis=1, keepdims=True)
        resid_grad[m] = cot_own[m] + scale_two[m] * (
            gain_two * back - resid[m] * scale_two[m] * mean_two
        )
        gain = jnp.sum(back * resid[m] * scale_two[m], axis=0)
        return col_gather(low(resid_grad[m])), gain

    back_a = start_back(first)
    back_b = start_back(second)
    advance(back_a, back_b)

    def ffn_grads(blocks, kind, kinds):
        held = line.hold(*turned)
        grads = ffn_grad_call(held, blocks, kind, kinds, row_count)
        line.mark(grads)
        grads = grads.reshape(kinds * hidden_col, width_all)
        return lax.psum_scatter(grads, "row", scatter_dimension=0, tiled=True)

    red_down = ffn_grads(cots, 2, 1)
    red_up = ffn_grads(normed_two, 0, 2)
    advance(back_a)
    low_a, gain_part = end_back(first, back_a)
    gain_two_sum = gain_two_sum + gain_part
    advance(back_b, low_a)
    low_b, gain_part = end_back(second, back_b)
    gain_two_sum = gain_two_sum + gain_part
    sum_a = start_ffn_sum(first)
    advance(low_a, low_b)

    projected_grads, resid_low, grads_input = [[None] * micro_count for _ in range(3)]
    tap_parts = [None] * micro_count
    gain_one_parts = [None] * micro_count

    def start_attention_back(m, stage):
        resid_low[m] = joined(finish(stage))
        grad_att = low(dot_nn(resid_low[m], out_full))
        grad_proj, tap_parts[m] = attend_back(
            inv, projected[m], grad_att, taps, links[m], segc[m], segr[m], feat_dim, head_dim
        )
        projected_grads[m] = grad_proj
        return col_scatter(*halves(lambda lo, hi: dot_nt(grad_proj[lo:hi], mix_full)))

    def end_input(m, stage):
        back = finish(stage)
        mean_one = jnp.mean(back * norm_one[m], axis=1, keepdims=True)
        grads_input[m] = resid_grad[m] + scale_one[m] * (
            gain_one * back - inputs[m] * scale_one[m] * mean_one
        )
        gain_one_parts[m] = jnp.sum(back * inputs[m] * scale_one[m], axis=0)
        line.mark(gain_one_parts[m])

    def end_ffn_sum(m, stage):
        outputs[m] = low(resid[m] + finish(stage))
        line.mark(outputs[m])

    (red_down,) = line.hold(red_down)
    line.mark(red_down)
    input_a = start_attention_back(first, low_a)
    advance(low_b, sum_a)
    input_b = start_attention_back(second, low_b)
    grad_projs = line.hold(*projected_grads)
    grad_both = low(
        jnp.concatenate(
            [
                sum(dot_tn(normed_one[m], grad_projs[m]) for m in micros),
                sum(dot_tn(resid_low[m], attended[m]) for m in micros),
            ],
            axis=1,
        )
    )
    line.mark(grad_both)
    advance(input_a, input_b, sum_a)
    sum_b = start_ffn_sum(second)
    red_up, grad_both = line.hold(red_up, grad_both)
    line.mark(grad_both)
    red_both = lax.psum_scatter(grad_both, "row", scatter_dimension=0, tiled=True)
    end_ffn_sum(first, sum_a)
    advance(input_a, sum_b, input_b)
    end_input(first, input_a)
    end_input(second, input_b)
    end_ffn_sum(second, sum_b)
    red_both = wide(red_both)
    red_mix, red_out = red_both[:, : heads * pack_dim], red_both[:, heads * pack_dim :]
    red_up = wide(red_up).reshape(2, hidden_own, width_all)
    red_down = wide(red_down)
    gain_one_sum = sum(gain_one_parts)
    tap_sum = sum(tap_parts)
    red_out = red_out.T.reshape(heads, LANES, block_d)[:, :head_dim].reshape(out_weight.shape)
    red_mix = red_mix.reshape(mix_weight.shape)
    tap_grads = tap_sum[:, :, :head_dim].transpose(1, 0, 2).reshape(tap_count, width_col)
    red_conv = sum_over(tap_grads, "row", row_count)
    red_gains = jnp.stack([gain_one_sum, gain_two_sum], axis=0)
    red_gains = sum_over(sum_over(red_gains, "col", col_count), "row", row_count)

    gain_means, gain_squares, new_gains = adam_update(
        norm_gains, red_gains, gain_mean, gain_square, VECTOR_RATE, 0.0
    )
    conv_means, conv_squares, new_kernel = adam_update(
        conv_kernel, red_conv, conv_mean, conv_square, VECTOR_RATE, 0.0
    )
    mix_means, mix_squares, new_mix = adam_update(
        mix_weight, red_mix, mix_mean, mix_square, D ** (-0.5), DECAY_RATE
    )
    out_means, out_squares, new_out = adam_update(
        out_weight, red_out, out_mean, out_square, 8.0 * D ** (-0.5), DECAY_RATE
    )
    up_means, up_squares, new_up = adam_update(
        up_weight, red_up, up_mean, up_square, D ** (-0.5), DECAY_RATE
    )
    down_means, down_squares, new_down = adam_update(
        down_weight, red_down, down_mean, down_square, FF ** (-0.5), DECAY_RATE
    )
    return (
        jnp.stack(outputs)[:, None],
        jnp.stack(grads_input)[:, None],
        gain_means,
        gain_squares,
        new_gains,
        conv_means,
        conv_squares,
        new_kernel,
        mix_means,
        mix_squares,
        new_mix,
        low(new_mix),
        out_means,
        out_squares,
        new_out,
        low(new_out),
        up_means,
        up_squares,
        new_up,
        low(new_up),
        down_means,
        down_squares,
        new_down,
        low(new_down),
    )


def solution(mesh):
    placed = (
        P(None, "row", "col", None),
        P(None, "row", "col", None),
        P(None, "row", None),
        P(),
        P(),
        P(),
        P(None, "col"),
        P(None, "col"),
        P(None, "col"),
        P("row", "col", None),
        P("row", "col", None),
        P("row", "col", None),
        P("col", "row"),
        P("col", "row"),
        P("col", "row"),
        P(None, ("row", "col"), None),
        P(None, ("row", "col"), None),
        P(None, ("row", "col"), None),
        P(("row", "col"), None),
        P(("row", "col"), None),
        P(("row", "col"), None),
    )
    return jax.shard_map(
        local,
        mesh=mesh,
        in_specs=placed,
        out_specs=(
            P(None, "row", "col", None),
            P(None, "row", "col", None),
            P(),
            P(),
            P(),
            P(None, "col"),
            P(None, "col"),
            P(None, "col"),
            P("row", "col", None),
            P("row", "col", None),
            P("row", "col", None),
            P("row", "col", None),
            P("col", "row"),
            P("col", "row"),
            P("col", "row"),
            P("col", "row"),
            P(None, ("row", "col"), None),
            P(None, ("row", "col"), None),
            P(None, ("row", "col"), None),
            P(None, ("row", "col"), None),
            P(("row", "col"), None),
            P(("row", "col"), None),
            P(("row", "col"), None),
            P(("row", "col"), None),
        ),
        check_vma=False,
    )
```

```python
import functools
import math

import jax
import jax.numpy as jnp
from jax import lax
from jax.experimental import pallas as pl
from jax.experimental.pallas import tpu as pltpu
from jax.sharding import PartitionSpec as P

D = 1792
FF = 4864
STEP = 10


NORM_EPSILON = 1e-05
BETA_ONE = 0.9
BETA_TWO = 0.95
ADAM_EPSILON = 1e-08
DECAY_RATE = 0.1
VECTOR_RATE = 0.5

LANES = 128
BLOCK_T = 256


def silu_grad(tensor):
    sigmoid_val = jax.nn.sigmoid(tensor)
    return sigmoid_val * (1.0 + tensor * (1.0 - sigmoid_val))


def low(tensor):
    return tensor.astype(jnp.bfloat16)


def wide(tensor):
    return tensor.astype(jnp.float32)


def dot_nn(left_side, right_side):
    return lax.dot_general(
        left_side, right_side, (((1,), (0,)), ((), ())), preferred_element_type=jnp.float32
    )


def dot_tn(left_side, right_side):
    return lax.dot_general(
        left_side, right_side, (((0,), (0,)), ((), ())), preferred_element_type=jnp.float32
    )


def dot_nt(left_side, right_side):
    return lax.dot_general(
        left_side, right_side, (((1,), (1,)), ((), ())), preferred_element_type=jnp.float32
    )


def row_scale(tensor):
    return lax.rsqrt(jnp.mean(tensor * tensor, axis=1, keepdims=True) + NORM_EPSILON)


def adam_update(weight, gradient, moment_one, moment_two, step_rate, decay_rate):
    first_new = BETA_ONE * moment_one + (1.0 - BETA_ONE) * gradient
    second_new = BETA_TWO * moment_two + (1.0 - BETA_TWO) * gradient * gradient
    first_hat = first_new / (1.0 - BETA_ONE**STEP)
    second_hat = second_new / (1.0 - BETA_TWO**STEP)
    weight_new = weight - step_rate * (
        first_hat / (jnp.sqrt(second_hat) + ADAM_EPSILON) + decay_rate * weight
    )
    return (first_new, second_new, weight_new)


def col_masks(col_count, core):
    bits = [1 << place for place in range(1, col_count.bit_length() - 1)]
    return bits if core == 0 else bits[::-1]


def chip_perm(col_count, step):
    return [(i, i ^ col_masks(col_count, i & 1)[step]) for i in range(col_count)]


def core_perm(col_count):
    return [(i, i ^ 1) for i in range(col_count)]


def col_steps(col_count):
    return col_count.bit_length() - 2


def slots_of_chunks(col_count):
    table = []
    for me in range(col_count):
        row = [0] * col_count
        for half in range(2):
            origin = me ^ half
            masks = col_masks(col_count, origin & 1)
            for slot in range(col_count // 2):
                chunk = origin
                for step, mask in enumerate(masks):
                    if slot >> step & 1:
                        chunk ^= mask
                row[chunk] = half * (col_count // 2) + slot
        table.append(row)
    return jnp.asarray(table, jnp.int32)[lax.axis_index("col")]


class Line:
    def __init__(self):
        self.marks = ()

    def hold(self, *arrays):
        return lax.optimization_barrier(arrays + self.marks)[: len(arrays)]

    def mark(self, *arrays):
        self.marks = arrays


class Stage:
    def __init__(self, steps):
        self.steps, self.ended, self.result = steps, False, None
        self.advance()

    def advance(self):
        if not self.ended:
            try:
                next(self.steps)
            except StopIteration as stop:
                self.ended, self.result = True, stop.value


def advance(*stages):
    for stage in stages:
        stage.advance()


def finish(stage):
    while not stage.ended:
        stage.advance()
    return stage.result


def gather_col(line, part, col_count):
    (held,) = line.hold(part)
    line.mark(held)
    arrived = lax.ppermute(held, "col", chip_perm(col_count, 0))
    for step in range(1, col_steps(col_count)):
        yield
        (arrived,) = line.hold(arrived)
        held = jnp.concatenate([held, arrived], axis=0)
        line.mark(held)
        arrived = lax.ppermute(held, "col", chip_perm(col_count, step))
    other_held = lax.ppermute(held, "col", core_perm(col_count))
    yield
    (arrived,) = line.hold(arrived)
    line.mark(arrived)
    other_arrived = lax.ppermute(arrived, "col", core_perm(col_count))
    yield
    other_held, other_arrived = line.hold(other_held, other_arrived)
    line.mark(other_held, other_arrived)
    return [held, arrived, other_held, other_arrived]


def scatter_col(line, own, other, col_count):
    line.mark(own, other)
    arrived = lax.ppermute(other, "col", core_perm(col_count))
    last_step = col_steps(col_count) - 1
    yield
    (arrived,) = line.hold(arrived)
    upper = low(wide(own[1]) + wide(arrived[1]))
    line.mark(upper)
    lower = arrived[0]
    arrived = lax.ppermute(upper, "col", chip_perm(col_count, last_step))
    yield
    arrived, lower = line.hold(arrived, lower)
    total = wide(own[0]) + wide(lower) + wide(arrived)
    for step in reversed(range(last_step)):
        rows = total.shape[0] // 2
        send = low(total[rows:])
        line.mark(send)
        arrived = lax.ppermute(send, "col", chip_perm(col_count, step))
        yield
        (arrived,) = line.hold(arrived)
        total = wide(total[:rows]) + wide(arrived)
    return total


def sum_over(tensor, axis, count):
    bit = 1
    while bit < count:
        tensor = tensor + lax.ppermute(tensor, axis, [(i, i ^ bit) for i in range(count)])
        bit *= 2
    return tensor


def head_parts(feat_dim, head_dim, inv_ref, proj_ref, proj_cols, taps, link_ref, p_ref):
    length = p_ref.shape[0]
    chunks = inv_ref.shape[0]
    rows = length // chunks
    for chunk in range(chunks):
        source = pl.multiple_of(inv_ref[chunk] * rows, rows)
        p_ref[chunk * rows : (chunk + 1) * rows, :] = proj_ref[pl.ds(source, rows), proj_cols]
    packed = p_ref[...]
    pack_dim = packed.shape[1]
    lane = lax.broadcasted_iota(jnp.int32, (length, LANES), 1)
    first = packed[:, :LANES]
    queries = low(jnp.where(lane < feat_dim, first, 0.0))
    keys = low(jnp.where(lane < feat_dim, pltpu.roll(first, LANES - feat_dim, 1), 0.0))
    inner = pltpu.roll(packed, pack_dim - 2 * feat_dim, 1)[:, :LANES]
    inner = jnp.where(lane < head_dim, inner, 0.0)
    gate = pltpu.roll(packed, pack_dim - 2 * feat_dim - head_dim, 1)[:, :LANES]
    gate = jnp.where(lane < head_dim, gate, 0.0)
    shifted = [inner]
    conv = taps[0:1, :] * inner
    for offset in range(1, taps.shape[0]):
        moved = pltpu.roll(inner, offset, 0)
        shifted.append(moved)
        conv = conv + taps[offset : offset + 1, :] * (moved * link_ref[:, offset : offset + 1])
    return queries, keys, gate, taps, shifted, conv


def kept_scores(feat_dim, block, keys, queries, segc_ref, segr_ref):
    first, last = block * BLOCK_T, (block + 1) * BLOCK_T
    score = dot_nt(keys[:last], queries[first:last]) * (1.0 / math.sqrt(feat_dim))
    key_at = lax.broadcasted_iota(jnp.int32, (last, BLOCK_T), 0)
    query_at = first + lax.broadcasted_iota(jnp.int32, (last, BLOCK_T), 1)
    kept = (key_at <= query_at) & (segc_ref[:last, :] == segr_ref[:, first:last])
    kern = jnp.where(kept, 1.0 + score + 0.5 * score * score, 0.0)
    scale = 1.0 / jnp.sum(kern, axis=0, keepdims=True)
    return score, kept, kern * scale, scale


def forward_kernel(
    feat_dim, head_dim, inv_ref, proj_ref, taps_ref, link_ref, segc_ref, segr_ref, out_ref, p_ref
):
    queries, keys, gate, taps, shifted, conv = head_parts(
        feat_dim, head_dim, inv_ref, proj_ref, slice(None), taps_ref[0], link_ref, p_ref
    )
    length = p_ref.shape[0]
    values = low(conv * (gate * jax.nn.sigmoid(gate))).T
    blocks = []
    for block in range(length // BLOCK_T):
        score, kept, probs, scale = kept_scores(
            feat_dim, block, keys, queries, segc_ref, segr_ref
        )
        last = (block + 1) * BLOCK_T
        blocks.append(low(dot_nn(values[:, :last], low(probs)).T))
    attended = jnp.concatenate(blocks, axis=0)
    chunks = inv_ref.shape[0]
    rows = length // chunks
    for chunk in range(chunks):
        target = pl.multiple_of(inv_ref[chunk] * rows, rows)
        out_ref[pl.ds(target, rows), :] = attended[chunk * rows : (chunk + 1) * rows]


def backward_kernel(feat_dim, head_dim, has_earlier, inv_ref, *refs):
    block_refs, refs = refs[:4], refs[4:]
    normed_ref, proj_ref, att_ref, weight_ref, taps_ref, link_ref, segc_ref, segr_ref = refs[:8]
    earlier_ref, refs = (refs[8], refs[9:]) if has_earlier else (None, refs[8:])
    own_ref, other_ref, sum_ref, tap_ref = refs[:4]
    p_ref, g_ref, dk_ref, dv_ref, resid_ref, att_grad_ref, packed_ref = refs[4:]
    heads = taps_ref.shape[0]
    length = p_ref.shape[0]
    pack_dim = p_ref.shape[1]
    packs = heads * pack_dim
    chunks = inv_ref.shape[0]
    rows = length // chunks
    block_rows = length // 4
    for block, ref in enumerate(block_refs):
        resid_ref[block * block_rows : (block + 1) * block_rows, :] = ref[...]
    att_grad_ref[...] = low(dot_nn(resid_ref[...], weight_ref[:, packs:]))
    root = 1.0 / math.sqrt(feat_dim)
    for head in range(heads):
        proj_cols = slice(head * pack_dim, (head + 1) * pack_dim)
        queries, keys, gate, taps, shifted, conv = head_parts(
            feat_dim, head_dim, inv_ref, proj_ref, proj_cols, taps_ref[head], link_ref, p_ref
        )
        for chunk in range(chunks):
            source = pl.multiple_of(inv_ref[chunk] * rows, rows)
            g_ref[chunk * rows : (chunk + 1) * rows, :] = att_grad_ref[
                pl.ds(source, rows), head * LANES : (head + 1) * LANES
            ]
        grad = g_ref[...]
        sigmoid_val = jax.nn.sigmoid(gate)
        gate_act = gate * sigmoid_val
        values = low(conv * gate_act)
        keys_turned = keys.T
        dk_ref[...] = jnp.zeros_like(dk_ref)
        dv_ref[...] = jnp.zeros_like(dv_ref)
        query_grads = []
        for block in range(length // BLOCK_T):
            first, last = block * BLOCK_T, (block + 1) * BLOCK_T
            score, kept, probs, scale = kept_scores(
                feat_dim, block, keys, queries, segc_ref, segr_ref
            )
            weight_grad = dot_nt(values[:last], grad[first:last])
            row_dot = jnp.sum(weight_grad * probs, axis=0, keepdims=True)
            score_grad = low(
                jnp.where(kept, (weight_grad - row_dot) * scale * (1.0 + score), 0.0)
            )
            query_grads.append(dot_nn(keys_turned[:, :last], score_grad).T)
            dk_ref[:last, :] += dot_nn(score_grad, queries[first:last])
            dv_ref[:last, :] += dot_nn(low(probs), grad[first:last])
        grad_queries = jnp.concatenate(query_grads, axis=0) * root
        grad_keys = dk_ref[...] * root
        grad_values = dv_ref[...]
        grad_conv = grad_values * gate_act
        grad_gate = grad_values * conv * (sigmoid_val * (1.0 + gate * (1.0 - sigmoid_val)))
        grad_inner = taps[0:1, :] * grad_conv
        tap_rows = [jnp.sum(grad_conv * shifted[0], axis=0, keepdims=True)]
        for offset in range(1, taps.shape[0]):
            masked = grad_conv * link_ref[:, offset : offset + 1]
            tap_rows.append(jnp.sum(masked * shifted[offset], axis=0, keepdims=True))
            grad_inner = grad_inner + taps[offset : offset + 1, :] * pltpu.roll(
                masked, length - offset, 0
            )
        for offset, tap_row in enumerate(tap_rows):
            tap_ref[head, offset : offset + 1, :] = tap_row
        empty = jnp.zeros((length, LANES), jnp.float32)
        packed = jnp.concatenate(
            [grad_queries + pltpu.roll(grad_keys, feat_dim, 1), empty], axis=1
        )
        packed = packed + pltpu.roll(
            jnp.concatenate([grad_inner, empty], axis=1), 2 * feat_dim, 1
        )
        packed = low(
            packed
            + pltpu.roll(jnp.concatenate([grad_gate, empty], axis=1), 2 * feat_dim + head_dim, 1)
        )
        for chunk in range(chunks):
            target = pl.multiple_of(inv_ref[chunk] * rows, rows)
            packed_ref[pl.ds(target, rows), proj_cols] = packed[chunk * rows : (chunk + 1) * rows]
    for block in range(4):
        ref = (own_ref, other_ref)[block // 2]
        ref[block % 2] = low(
            dot_nt(
                packed_ref[block * block_rows : (block + 1) * block_rows, :],
                weight_ref[:, :packs],
            )
        )
    mix_sum = dot_tn(normed_ref[...], packed_ref[...])
    out_sum = dot_tn(resid_ref[...], att_ref[...])
    if has_earlier:
        mix_sum = mix_sum + wide(earlier_ref[:, :packs])
        out_sum = out_sum + wide(earlier_ref[:, packs:])
    sum_ref[:, :packs] = low(mix_sum)
    sum_ref[:, packs:] = low(out_sum)


def whole_spec(shape):
    return pl.BlockSpec(shape, lambda head, inv: (0,) * len(shape))


def attend(inv, projected, taps, links, segc, segr, feat_dim, head_dim):
    length = projected.shape[0]
    heads, tap_count = taps.shape[0], taps.shape[1]
    pack_dim = projected.shape[1] // heads
    return pl.pallas_call(
        functools.partial(forward_kernel, feat_dim, head_dim),
        out_shape=jax.ShapeDtypeStruct((length, heads * LANES), jnp.bfloat16),
        grid_spec=pltpu.PrefetchScalarGridSpec(
            num_scalar_prefetch=1,
            grid=(heads,),
            in_specs=[
                pl.BlockSpec((length, pack_dim), lambda head, inv: (0, head)),
                pl.BlockSpec((1, tap_count, LANES), lambda head, inv: (head, 0, 0)),
                whole_spec(links.shape),
                whole_spec(segc.shape),
                whole_spec(segr.shape),
            ],
            out_specs=pl.BlockSpec((length, LANES), lambda head, inv: (0, head)),
            scratch_shapes=[pltpu.VMEM((length, pack_dim), jnp.float32)],
        ),
        compiler_params=pltpu.CompilerParams(vmem_limit_bytes=40 * 1024 * 1024),
        cost_estimate=pl.CostEstimate(
            flops=heads * length * length * LANES * 3,
            bytes_accessed=heads * length * (pack_dim * 4 + LANES * 2),
            transcendentals=heads * length * LANES,
        ),
    )(inv, projected, taps, links, segc, segr)


def attend_back(
    inv, blocks, normed, projected, attended, weights, taps, links, segc, segr, earlier, sizes
):
    length, width = normed.shape
    heads, tap_count = taps.shape[0], taps.shape[1]
    pack_dim = projected.shape[1] // heads
    operands = [*blocks, normed, projected, attended, weights, taps, links, segc, segr]
    operands += [] if earlier is None else [earlier]
    half = jax.ShapeDtypeStruct((2, length // 4, width), jnp.bfloat16)
    vmem = pl.BlockSpec(memory_space=pltpu.VMEM)
    return pl.pallas_call(
        functools.partial(backward_kernel, *sizes, earlier is not None),
        in_specs=[pl.BlockSpec(memory_space=pltpu.SMEM)] + [vmem] * len(operands),
        out_specs=(vmem,) * 4,
        out_shape=(
            half,
            half,
            jax.ShapeDtypeStruct(weights.shape, jnp.bfloat16),
            jax.ShapeDtypeStruct((heads, tap_count, LANES), jnp.float32),
        ),
        scratch_shapes=[
            pltpu.VMEM((length, pack_dim), jnp.float32),
            pltpu.VMEM((length, LANES), jnp.bfloat16),
            pltpu.VMEM((length, LANES), jnp.float32),
            pltpu.VMEM((length, LANES), jnp.float32),
            pltpu.VMEM((length, width), jnp.bfloat16),
            pltpu.VMEM((length, heads * LANES), jnp.bfloat16),
            pltpu.VMEM((length, heads * pack_dim), jnp.bfloat16),
        ],
        compiler_params=pltpu.CompilerParams(vmem_limit_bytes=56 * 1024 * 1024),
        cost_estimate=pl.CostEstimate(
            flops=heads * length * (length * LANES * 6 + 6 * width * (pack_dim + LANES)),
            bytes_accessed=10 * length * width,
            transcendentals=heads * length * LANES,
        ),
    )(inv, *operands)


def ffn_kernel(*refs):
    normed_refs, cot_refs = refs[:4], refs[4:8]
    weight_ref, turned_ref, own_ref, other_ref = refs[8:]
    hidden, width = weight_ref.shape[1:]
    rows = normed_refs[0].shape[0]
    normed = jnp.concatenate([ref[...] for ref in normed_refs], axis=0)
    cot = jnp.concatenate([ref[...] for ref in cot_refs], axis=0)
    gate = dot_nt(weight_ref[0], normed)
    up = dot_nt(weight_ref[1], normed)
    grad_hidden = dot_nt(weight_ref[2], cot)
    sigmoid_val = jax.nn.sigmoid(gate)
    gate_sig = gate * sigmoid_val
    turned_ref[0] = low(grad_hidden * up * (sigmoid_val * (1.0 + gate * (1.0 - sigmoid_val))))
    turned_ref[1] = low(grad_hidden * gate_sig)
    turned_ref[2] = low(gate_sig * up)
    back = low(
        dot_tn(
            turned_ref[:2].reshape(2 * hidden, 4 * rows), weight_ref[:2].reshape(2 * hidden, width)
        )
    )
    for block, ref in enumerate((own_ref, own_ref, other_ref, other_ref)):
        ref[block % 2] = back[block * rows : (block + 1) * rows]


def ffn_call(normed, cot, weights):
    block_rows, width = normed[0].shape
    _, hidden, _ = weights.shape
    rows = block_rows // 2
    block = pl.BlockSpec((rows, width), lambda step: (step, 0))
    half = pl.BlockSpec((2, rows, width), lambda step: (0, step, 0))
    return pl.pallas_call(
        ffn_kernel,
        grid=(block_rows // rows,),
        in_specs=[block] * 8
        + [
            pl.BlockSpec(
                weights.shape, lambda step: (0, 0, 0), pipeline_mode=pl.Buffered(buffer_count=1)
            )
        ],
        out_specs=(
            pl.BlockSpec((3, hidden, 4 * rows), lambda step: (0, 0, step)),
            half,
            half,
        ),
        out_shape=(
            jax.ShapeDtypeStruct((3, hidden, 4 * block_rows), jnp.bfloat16),
            jax.ShapeDtypeStruct((2, block_rows, width), jnp.bfloat16),
            jax.ShapeDtypeStruct((2, block_rows, width), jnp.bfloat16),
        ),
        compiler_params=pltpu.CompilerParams(vmem_limit_bytes=52 * 1024 * 1024),
        cost_estimate=pl.CostEstimate(
            flops=2 * 5 * 4 * block_rows * hidden * width,
            bytes_accessed=2 * (3 * hidden * width + 12 * block_rows * width),
            transcendentals=4 * block_rows * hidden,
        ),
    )(*normed, *cot, weights)


def ffn_sum_kernel(hidden_ref, weight_ref, own_ref, other_ref):
    rows = own_ref.shape[1]
    total = low(dot_tn(hidden_ref[0], weight_ref[0]))
    for block, ref in enumerate((own_ref, own_ref, other_ref, other_ref)):
        ref[block % 2] = total[block * rows : (block + 1) * rows]


def ffn_sum_call(turned, weights):
    _, hidden, tokens = turned.shape
    width = weights.shape[2]
    rows = tokens // 8
    half = pl.BlockSpec((2, rows, width), lambda step: (0, step, 0))
    shape = jax.ShapeDtypeStruct((2, tokens // 4, width), jnp.bfloat16)
    return pl.pallas_call(
        ffn_sum_kernel,
        grid=(2,),
        in_specs=[
            pl.BlockSpec((1, hidden, 4 * rows), lambda step: (2, 0, step)),
            pl.BlockSpec((1, hidden, width), lambda step: (2, 0, 0)),
        ],
        out_specs=(half, half),
        out_shape=(shape, shape),
        compiler_params=pltpu.CompilerParams(vmem_limit_bytes=40 * 1024 * 1024),
        cost_estimate=pl.CostEstimate(
            flops=2 * tokens * hidden * width,
            bytes_accessed=2 * (hidden * width + tokens * (hidden + width)),
            transcendentals=0,
        ),
    )(turned, weights)


def ffn_grad_kernel(micro_count, steps, *refs):
    turned_refs, block_refs, out_ref = refs[:micro_count], refs[micro_count:-1], refs[-1]
    owners, kinds, own, _ = out_ref.shape
    hidden = owners * own
    rows = block_refs[0].shape[0] // steps
    total = None
    for micro, turned_ref in enumerate(turned_refs):
        tokens = jnp.concatenate(
            [
                ref[step * rows : (step + 1) * rows, :]
                for step in range(steps)
                for ref in block_refs[4 * micro : 4 * micro + 4]
            ],
            axis=0,
        )
        part = dot_nn(turned_ref[...].reshape(kinds * hidden, turned_ref.shape[2]), tokens)
        total = part if total is None else total + part
    for owner in range(owners):
        for kind in range(kinds):
            first = kind * hidden + owner * own
            out_ref[owner, kind] = low(total[first : first + own])


def ffn_grad_call(turned, blocks, first, kinds, owners):
    micro_count = len(turned)
    _, hidden, tokens = turned[0].shape
    block_rows, width = blocks[0][0].shape
    lanes = 2 * LANES
    return pl.pallas_call(
        functools.partial(ffn_grad_kernel, micro_count, 2),
        grid=(width // lanes,),
        in_specs=[
            pl.BlockSpec(
                (kinds, hidden, tokens),
                lambda step: (first // kinds, 0, 0),
                pipeline_mode=pl.Buffered(buffer_count=1),
            )
        ]
        * micro_count
        + [pl.BlockSpec((block_rows, lanes), lambda step: (0, step))] * (4 * micro_count),
        out_specs=pl.BlockSpec(
            (owners, kinds, hidden // owners, lanes), lambda step: (0, 0, 0, step)
        ),
        out_shape=jax.ShapeDtypeStruct((owners, kinds, hidden // owners, width), jnp.bfloat16),
        compiler_params=pltpu.CompilerParams(vmem_limit_bytes=52 * 1024 * 1024),
        cost_estimate=pl.CostEstimate(
            flops=2 * kinds * micro_count * tokens * hidden * width,
            bytes_accessed=2 * (kinds * hidden * (width + tokens) + micro_count * tokens * width),
            transcendentals=0,
        ),
    )(*turned, *[block for group in blocks for block in group])


def local(
    layer_input,
    cotangent,
    segments,
    norm_gains,
    gain_mean,
    gain_square,
    conv_kernel,
    conv_mean,
    conv_square,
    mix_weight,
    mix_mean,
    mix_square,
    out_weight,
    out_mean,
    out_square,
    up_weight,
    up_mean,
    up_square,
    down_weight,
    down_mean,
    down_square,
):
    micro_count = layer_input.shape[0]
    length = segments.shape[2]
    width_all = layer_input.shape[3]
    block_d, heads, pack_dim = mix_weight.shape
    width_col = out_weight.shape[0]
    head_dim = width_col // heads
    feat_dim = (pack_dim - 2 * head_dim) // 2
    tap_count = conv_kernel.shape[0]
    row_count = lax.axis_size("row")
    col_count = lax.axis_size("col")
    hidden_own = down_weight.shape[0]
    hidden_col = hidden_own * row_count
    row_me = lax.axis_index("row")
    inv = slots_of_chunks(col_count)
    micros = range(micro_count)
    gain_one, gain_two = norm_gains[0], norm_gains[1]

    mix_own = low(mix_weight).reshape(block_d, heads * pack_dim)
    out_own = jnp.pad(
        low(out_weight).reshape(heads, head_dim, block_d), ((0, 0), (0, LANES - head_dim), (0, 0))
    )
    out_own = out_own.reshape(heads * LANES, block_d).T
    mix_out_own = jnp.concatenate([mix_own, out_own], axis=1)
    mix_out = lax.all_gather(mix_out_own, "row", axis=0, tiled=True)
    mix_full, out_full = mix_out[:, : heads * pack_dim], mix_out[:, heads * pack_dim :]
    ffn_own = low(jnp.concatenate([up_weight, down_weight[None]], axis=0))
    ffn_full = lax.all_gather(ffn_own, "row", axis=1, tiled=True)

    taps = jnp.pad(
        conv_kernel.reshape(tap_count, heads, head_dim).transpose(1, 0, 2),
        ((0, 0), (0, 0), (0, LANES - head_dim)),
    )

    def links_of(segs):
        columns = [jnp.ones((length,), jnp.float32)]
        for offset in range(1, tap_count):
            earlier = jnp.concatenate(
                [jnp.full((offset,), -1, jnp.int32), segs[: length - offset]]
            )
            columns.append((earlier == segs).astype(jnp.float32))
        return jnp.stack(columns, axis=1)

    inputs = [wide(layer_input[m, 0]) for m in micros]
    scale_one = [row_scale(x) for x in inputs]
    norm_one = [x * s * gain_one for x, s in zip(inputs, scale_one)]
    cot_own = [wide(cotangent[m, 0]) for m in micros]
    segs = [segments[m, 0] for m in micros]
    links = [links_of(sg) for sg in segs]
    segc = [sg[:, None] for sg in segs]
    segr = [sg[None, :] for sg in segs]
    first, second = micros[0], micros[-1]
    line = Line()

    def col_gather(part):
        return Stage(gather_col(line, part, col_count))

    def col_scatter(own, other):
        return Stage(scatter_col(line, own, other, col_count))

    def halves(product):
        half, rows = length // 2, length // 4
        own, other = low(product(0, half)), low(product(half, length))
        return own.reshape(2, rows, width_all), other.reshape(2, rows, width_all)

    def joined(blocks):
        full = jnp.concatenate(blocks, axis=0)
        line.mark(full)
        return full

    def start_attention(m):
        normed, mix = line.hold(normed_one[m], mix_full)
        proj = dot_nn(normed, mix)
        att = attend(inv, proj, taps, links[m], segc[m], segr[m], feat_dim, head_dim)
        projected[m], attended[m] = proj, att
        return col_scatter(*halves(lambda lo, hi: dot_nt(att[lo:hi], out_full)))

    def end_mixer(m, stage):
        resid[m] = inputs[m] + finish(stage)
        scale_two[m] = row_scale(resid[m])
        norm_two[m] = resid[m] * scale_two[m] * gain_two
        return col_gather(low(norm_two[m]))

    normed_one, cots, projected, attended, resid, scale_two, norm_two, normed_two = [
        [None] * micro_count for _ in range(8)
    ]

    one_a = col_gather(low(norm_one[first]))
    line.mark(*line.marks, ffn_own)
    advance(one_a)
    one_b = col_gather(low(norm_one[second]))
    advance(one_b, one_a)
    cot_a = col_gather(cotangent[first, 0])
    normed_one[first] = joined(finish(one_a))
    advance(one_b, cot_a)
    normed_one[second] = joined(finish(one_b))
    mix_a = start_attention(first)
    advance(cot_a)
    cot_b = col_gather(cotangent[second, 0])
    mix_b = start_attention(second)
    advance(mix_a, cot_b, mix_b)
    cots[first] = finish(cot_a)
    advance(mix_a, cot_b, mix_b)
    two_a = end_mixer(first, mix_a)
    two_b = end_mixer(second, mix_b)
    advance(two_a)
    cots[second] = finish(cot_b)
    advance(two_b)
    advance(two_a)
    normed_two[first] = finish(two_a)
    advance(two_b)
    (ffn_full,) = line.hold(ffn_full)
    line.mark(ffn_full)
    normed_two[second] = finish(two_b)

    turned, resid_grad, outputs = [[None] * micro_count for _ in range(3)]

    def start_back(m):
        held = line.hold(*normed_two[m], *cots[m])
        turned[m], own, other = ffn_call(held[:4], held[4:], ffn_full)
        return col_scatter(own, other)

    def start_ffn_sum(m):
        (held,) = line.hold(turned[m])
        return col_scatter(*ffn_sum_call(held, ffn_full))

    gain_two_sum = 0.0

    def end_back(m, stage):
        back = finish(stage)
        mean_two = jnp.mean(back * norm_two[m], axis=1, keepdims=True)
        resid_grad[m] = cot_own[m] + scale_two[m] * (
            gain_two * back - resid[m] * scale_two[m] * mean_two
        )
        gain = jnp.sum(back * resid[m] * scale_two[m], axis=0)
        return col_gather(low(resid_grad[m])), gain

    back_a = start_back(first)
    back_b = start_back(second)
    advance(back_a, back_b)

    def ffn_grads(blocks, kind, kinds):
        held = line.hold(*turned)
        grads = ffn_grad_call(held, blocks, kind, kinds, row_count)
        line.mark(grads)
        grads = grads.reshape(kinds * hidden_col, width_all)
        return lax.psum_scatter(grads, "row", scatter_dimension=0, tiled=True)

    red_down = ffn_grads(cots, 2, 1)
    red_gate = ffn_grads(normed_two, 0, 1)
    red_up = ffn_grads(normed_two, 1, 1)
    advance(back_a)
    low_a, gain_part = end_back(first, back_a)
    gain_two_sum = gain_two_sum + gain_part
    advance(back_b, low_a)
    low_b, gain_part = end_back(second, back_b)
    gain_two_sum = gain_two_sum + gain_part
    advance(low_a, low_b)

    grads_input = [None] * micro_count
    tap_parts = [None] * micro_count
    gain_one_parts = [None] * micro_count

    def start_attention_back(m, stage, earlier):
        blocks = line.hold(*finish(stage))
        own, other, sums, tap_parts[m] = attend_back(
            inv,
            blocks,
            normed_one[m],
            projected[m],
            attended[m],
            mix_out,
            taps,
            links[m],
            segc[m],
            segr[m],
            earlier,
            (feat_dim, head_dim),
        )
        return col_scatter(own, other), sums

    def end_input(m, stage):
        back = finish(stage)
        mean_one = jnp.mean(back * norm_one[m], axis=1, keepdims=True)
        grads_input[m] = resid_grad[m] + scale_one[m] * (
            gain_one * back - inputs[m] * scale_one[m] * mean_one
        )
        gain_one_parts[m] = jnp.sum(back * inputs[m] * scale_one[m], axis=0)
        line.mark(gain_one_parts[m])

    def end_ffn_sum(m, stage):
        outputs[m] = low(resid[m] + finish(stage))
        line.mark(outputs[m])

    (red_down,) = line.hold(red_down)
    line.mark(red_down)
    input_a, sums = start_attention_back(first, low_a, None)
    sum_a = start_ffn_sum(first)
    advance(low_b)
    (red_gate,) = line.hold(red_gate)
    line.mark(red_gate)
    input_b, sums = start_attention_back(second, low_b, sums)
    sum_b = start_ffn_sum(second)
    advance(input_a, sum_a, input_b, sum_b)
    red_up, sums = line.hold(red_up, sums)
    line.mark(sums)
    red_both = lax.psum_scatter(sums, "row", scatter_dimension=0, tiled=True)
    advance(input_a, sum_a, input_b, sum_b)
    end_input(first, input_a)
    end_ffn_sum(first, sum_a)
    end_input(second, input_b)
    end_ffn_sum(second, sum_b)
    red_both = wide(red_both)
    red_mix, red_out = red_both[:, : heads * pack_dim], red_both[:, heads * pack_dim :]
    red_up = wide(jnp.stack([red_gate, red_up], axis=0))
    red_down = wide(red_down)
    gain_one_sum = sum(gain_one_parts)
    tap_sum = sum(tap_parts)
    red_out = red_out.T.reshape(heads, LANES, block_d)[:, :head_dim].reshape(out_weight.shape)
    red_mix = red_mix.reshape(mix_weight.shape)
    tap_grads = tap_sum[:, :, :head_dim].transpose(1, 0, 2).reshape(tap_count, width_col)
    red_conv = sum_over(tap_grads, "row", row_count)
    red_gains = jnp.stack([gain_one_sum, gain_two_sum], axis=0)
    red_gains = sum_over(sum_over(red_gains, "col", col_count), "row", row_count)

    gain_means, gain_squares, new_gains = adam_update(
        norm_gains, red_gains, gain_mean, gain_square, VECTOR_RATE, 0.0
    )
    conv_means, conv_squares, new_kernel = adam_update(
        conv_kernel, red_conv, conv_mean, conv_square, VECTOR_RATE, 0.0
    )
    mix_means, mix_squares, new_mix = adam_update(
        mix_weight, red_mix, mix_mean, mix_square, D ** (-0.5), DECAY_RATE
    )
    out_means, out_squares, new_out = adam_update(
        out_weight, red_out, out_mean, out_square, 8.0 * D ** (-0.5), DECAY_RATE
    )
    up_means, up_squares, new_up = adam_update(
        up_weight, red_up, up_mean, up_square, D ** (-0.5), DECAY_RATE
    )
    down_means, down_squares, new_down = adam_update(
        down_weight, red_down, down_mean, down_square, FF ** (-0.5), DECAY_RATE
    )
    return (
        jnp.stack(outputs)[:, None],
        jnp.stack(grads_input)[:, None],
        gain_means,
        gain_squares,
        new_gains,
        conv_means,
        conv_squares,
        new_kernel,
        mix_means,
        mix_squares,
        new_mix,
        low(new_mix),
        out_means,
        out_squares,
        new_out,
        low(new_out),
        up_means,
        up_squares,
        new_up,
        low(new_up),
        down_means,
        down_squares,
        new_down,
        low(new_down),
    )


def solution(mesh):
    placed = (
        P(None, "row", "col", None),
        P(None, "row", "col", None),
        P(None, "row", None),
        P(),
        P(),
        P(),
        P(None, "col"),
        P(None, "col"),
        P(None, "col"),
        P("row", "col", None),
        P("row", "col", None),
        P("row", "col", None),
        P("col", "row"),
        P("col", "row"),
        P("col", "row"),
        P(None, ("row", "col"), None),
        P(None, ("row", "col"), None),
        P(None, ("row", "col"), None),
        P(("row", "col"), None),
        P(("row", "col"), None),
        P(("row", "col"), None),
    )
    return jax.shard_map(
        local,
        mesh=mesh,
        in_specs=placed,
        out_specs=(
            P(None, "row", "col", None),
            P(None, "row", "col", None),
            P(),
            P(),
            P(),
            P(None, "col"),
            P(None, "col"),
            P(None, "col"),
            P("row", "col", None),
            P("row", "col", None),
            P("row", "col", None),
            P("row", "col", None),
            P("col", "row"),
            P("col", "row"),
            P("col", "row"),
            P("col", "row"),
            P(None, ("row", "col"), None),
            P(None, ("row", "col"), None),
            P(None, ("row", "col"), None),
            P(None, ("row", "col"), None),
            P(("row", "col"), None),
            P(("row", "col"), None),
            P(("row", "col"), None),
            P(("row", "col"), None),
        ),
        check_vma=False,
    )
```
